256 devices in a mesh: dp: 16 (over z_hi, y, core), fsdp: 16 (over x, z_lo).
Axes of the slice: x: 4, y: 4, z: 8 (z_hi: 2, z_lo: 4; z = z_hi * 4 + z_lo), core: 2. Of those that a mesh axis runs over, the one named last changes fastest.
Arguments:
- gradient: bfloat16 [16, 16, 896, 4096], P('dp', None, 'fsdp'), may hold values from -6 to 6
- projector: bfloat16 [4096, 1024], P('fsdp'), may hold values from -0.09375 to 0.09375
- first_moment: float32 [16, 896, 1024], P('dp', 'fsdp'), may hold values from -4 to 4
- second_moment: float32 [16, 896, 1024], P('dp', 'fsdp'), may hold values from 0.002 to 0.05
Outputs:
- update: bfloat16 [16, 896, 4096], P('dp', None, 'fsdp')
- new_first: float32 [16, 896, 1024], P('dp', 'fsdp')
- new_second: float32 [16, 896, 1024], P('dp', 'fsdp')
The draws below stay inside these ranges and needn't reach their ends.
All inputs are finite; a program needn't handle non-finite values.
Results may differ from the reference program's by a relative error of at most 0.0048.
Values may be sent and summed in bfloat16 or wider, within the bound.
No kernel may reach another device: no remote copies, remote signals or barrier semaphores. Data moves between devices by JAX's collectives and lax.ppermute only.
A program may use at most 64 MiB of HBM per device.

```python
import math
import jax
import jax.numpy as jnp
from jax import lax

D = 4096
RANK = 1024
ROWB = 896
N_DP = 16


def spiked(result, rng, source, target, shards_of, factor):
    def block_of(position):
        return (jnp.arange(result.shape[position]) // (result.shape[position] // shards_of)).reshape((-1,) + (1,) * (result.ndim - 1 - position))

    one_side = jax.random.permutation(rng, shards_of)[block_of(target)]
    other_side = (block_of(target) + shards_of // 2) % shards_of
    return jnp.where((block_of(source) == one_side) | (block_of(source) == other_side), factor * result, result)


def block_levels(stream_key, shape, cuts, smallest, largest):
    loudness = 1.0
    for position, blocks in cuts:
        heights = jax.random.uniform(jax.random.fold_in(jax.random.fold_in(stream_key, 6), position), (blocks,), jnp.float32, smallest / len(cuts), largest / len(cuts))
        loudness = loudness * jnp.repeat(jnp.exp(heights), shape[position] // blocks).reshape((-1,) + (1,) * (len(shape) - 1 - position))
    return loudness


def normal_values(rng, extent, scale, reach, pieces=(), kind=jnp.bfloat16):
    factor_of = block_levels(rng, extent, pieces, -0.22, 0.18) if pieces else 1.0
    result = jax.random.normal(rng, extent, jnp.float32) * scale * factor_of
    return jnp.minimum(jnp.maximum(result, -reach), reach).astype(kind)


def gaussian_with(own_key, shape, scale, bound, pieces, heavy, kind=jnp.bfloat16):
    result = scale * jax.random.normal(own_key, shape, jnp.float32)
    if pieces:
        result = result * block_levels(own_key, shape, pieces, -0.22, 0.18)
    return jnp.clip(spiked(result, jax.random.fold_in(own_key, 3), *heavy), -bound, bound).astype(kind)


def setup_inputs(seed: int = 0) -> dict:
    arg_keys = jax.random.split(jax.random.key(seed), 5)
    gradient = gaussian_with(arg_keys[0], (N_DP, N_DP, ROWB, D), 1.0, 6.0, ((0, 16), (2, 16)), (0, 1, 16, 2.0))
    projector = normal_values(arg_keys[1], (D, RANK), D ** -0.5, 0.09375, ((0, 16),))
    first_moment = normal_values(arg_keys[2], (N_DP, ROWB, RANK), 0.3, 4.0, ((0, 16), (1, 16)), jnp.float32)
    second_moment = jnp.clip(jnp.exp(math.log(0.05) - 3.218876 * jax.random.uniform(arg_keys[3], (N_DP, ROWB, RANK), jnp.float32) ** block_levels(arg_keys[3], (N_DP, ROWB, RANK), ((0, 16), (1, 16)), -0.2, 0.2)), 0.002, 0.05)
    return dict(gradient=gradient, projector=projector, first_moment=first_moment, second_moment=second_moment)


beta_one = 0.9
beta_two = 0.999
bias_one = 1.0 - 0.9 ** 10
bias_two = 1.0 - 0.999 ** 10
epsilon = 1e-08

def reference(gradient, projector, first_moment, second_moment):
    projected = jnp.zeros((N_DP * ROWB, RANK), jnp.float32)
    for replica in range(N_DP):
        rows = gradient[replica].reshape(N_DP * ROWB, D)
        projected = projected + jnp.dot(rows, projector, preferred_element_type=jnp.float32)
    projected = projected.reshape(N_DP, ROWB, RANK)
    new_first = beta_one * first_moment + (1.0 - beta_one) * projected
    new_second = beta_two * second_moment + (1.0 - beta_two) * projected * projected
    direction = new_first / bias_one / (jnp.sqrt(new_second / bias_two) + epsilon)
    direction = direction.astype(jnp.bfloat16).reshape(N_DP * ROWB, RANK)
    update = lax.dot_general(direction, projector, (((1,), (1,)), ((), ())), preferred_element_type=jnp.float32)
    update = update.astype(jnp.bfloat16).reshape(N_DP, ROWB, D)
    return (update, new_first, new_second)
```

```python
import functools

import jax
import jax.numpy as jnp
from jax import lax
from jax.experimental import pallas as pl
from jax.experimental.pallas import tpu as pltpu
from jax.sharding import PartitionSpec as P

beta_one = 0.9
beta_two = 0.999
bias_one = 1.0 - 0.9**10
bias_two = 1.0 - 0.999**10
epsilon = 1e-08

ZH, Y, C, X, ZL = 2, 4, 2, 4, 4
AXES = ("dp", "fsdp")
OFFSETS = (0, 1, -1, 2)
GROUPS = 1


def linear(zh, y, c, x, zl):
    return (((zh * Y + y) * C + c) * X + x) * ZL + zl


def move(value, place):
    pairs = []
    for zh in range(ZH):
        for y in range(Y):
            for c in range(C):
                for x in range(X):
                    for zl in range(ZL):
                        target = place(zh, y, c, x, zl)
                        pairs.append((linear(zh, y, c, x, zl), linear(*target)))
    return lax.ppermute(value, AXES, pairs)


def along_x(step):
    return lambda zh, y, c, x, zl: (zh, y, c, (x + step) % X, zl)


def along_y(step):
    return lambda zh, y, c, x, zl: (zh, (y + step) % Y, c, x, zl)


def along_ring(step):
    def place(zh, y, c, x, zl):
        z = (zh * ZL + zl + step) % (ZH * ZL)
        return (z // ZL, y, c, x, z % ZL)

    return place


def along_line(step):
    return lambda zh, y, c, x, zl: (zh, y, c, x, (zl + step) % ZL)


def other_core(zh, y, c, x, zl):
    return (zh, y, 1 - c, x, zl)


def other_half(zh, y, c, x, zl):
    return (1 - zh, y, c, x, zl)


def by_core(first, second):
    def place(zh, y, c, x, zl):
        return (first if c == 0 else second)(zh, y, c, x, zl)

    return place


def project_kernel(pieces, last, has_acc, order, *refs):
    lefts = refs[: 2 * pieces]
    rights = refs[2 * pieces : 3 * pieces]
    rest = refs[3 * pieces :]
    if has_acc:
        acc_in, rest = rest[0], rest[1:]
    outs, total = rest[:-1], rest[-1]
    step = pl.program_id(0)
    steps = pl.num_programs(0)
    rows = total.shape[0]
    chunk = rows // 4
    for part in range(4):
        at = pl.ds(part * chunk, chunk)
        value = None
        for piece in range(pieces):
            basis = rights[piece][0]
            for side in range(2):
                term = jnp.dot(
                    lefts[2 * piece + side][at, :],
                    basis,
                    preferred_element_type=jnp.float32,
                )
                value = term if value is None else value + term

        @pl.when(step == 0)
        def _():
            if has_acc:
                total[at, :] = acc_in[at, :] + value
            else:
                total[at, :] = value

        @pl.when(step > 0)
        def _():
            total[at, :] += value

    @pl.when(step == steps - 1)
    def _():
        if not last:
            outs[0][...] = total[...]
        else:
            base = pieces * steps
            band = rows // (ZH * Y)
            for dy in range(Y):
                for half in range(ZH):
                    row = order[base + dy * ZH + half] * band
                    value = total[pl.ds(pl.multiple_of(row, 16), band), :]
                    outs[dy][half] = value.astype(outs[dy].dtype)


def project(order, grads, rights, acc, last):
    pieces = len(rights)
    steps, depth, width = rights[0].shape
    rows = grads[0].shape[0]
    in_specs = []
    operands = []
    for piece in range(pieces):
        for side in range(2):
            in_specs.append(
                pl.BlockSpec(
                    (rows, depth),
                    functools.partial(
                        lambda first, i, order: (0, order[first + i]), piece * steps
                    ),
                )
            )
            operands.append(grads[side])
    for right in rights:
        in_specs.append(pl.BlockSpec((1, depth, width), lambda i, order: (i, 0, 0)))
        operands.append(right)
    if acc is not None:
        in_specs.append(pl.BlockSpec((rows, width), lambda i, order: (0, 0)))
        operands.append(acc)
    if last:
        band = rows // (ZH * Y)
        shapes = [
            jax.ShapeDtypeStruct(
                (ZH, band, width), jnp.float32 if dy == 0 else jnp.bfloat16
            )
            for dy in range(Y)
        ]
        out_specs = [
            pl.BlockSpec((ZH, band, width), lambda i, order: (0, 0, 0))
            for _ in range(Y)
        ]
    else:
        shapes = [jax.ShapeDtypeStruct((rows, width), jnp.float32)]
        out_specs = [pl.BlockSpec((rows, width), lambda i, order: (0, 0))]
    return pl.pallas_call(
        functools.partial(project_kernel, pieces, last, acc is not None),
        out_shape=shapes,
        grid_spec=pltpu.PrefetchScalarGridSpec(
            num_scalar_prefetch=1,
            grid=(steps,),
            in_specs=in_specs,
            out_specs=out_specs,
            scratch_shapes=[pltpu.VMEM((rows, width), jnp.float32)],
        ),
        compiler_params=pltpu.CompilerParams(
            dimension_semantics=("arbitrary",), vmem_limit_bytes=28 * 1024 * 1024
        ),
        cost_estimate=pl.CostEstimate(
            flops=4 * pieces * steps * rows * depth * width,
            bytes_accessed=2 * pieces * steps * depth * (2 * rows + width)
            + 8 * rows * width,
            transcendentals=0,
        ),
    )(order, *operands)


def per_device(gradient, projector, first_moment, second_moment):
    blocks = gradient.shape[1]
    owned = gradient.shape[2]
    width = gradient.shape[3]
    depth, rank_cols = projector.shape
    half = rank_cols // 2
    part = half // GROUPS
    rows = blocks * owned
    dp = lax.axis_index("dp")
    fsdp = lax.axis_index("fsdp")
    zh, y, c = dp // (Y * C), (dp // C) % Y, dp % C
    x, zl = fsdp // ZL, fsdp % ZL

    own_grad = gradient.reshape(rows, width)
    grads = (own_grad, move(own_grad, other_core))
    own_half = lax.dynamic_slice(projector, (0, c * half), (depth, half))

    def column(inner, outer):
        dx = jnp.where(c == 0, inner, outer)
        dz = jnp.where(c == 0, outer, inner)
        return ((x + dx) % X) * ZL + (zl + dz) % ZL

    bands = [
        h * Y + (y + OFFSETS[dy]) % Y for dy in range(Y) for h in (zh, 1 - zh)
    ]
    order_a = jnp.stack([column(i, 0) for i in OFFSETS])
    order_b = jnp.stack([column(i, o) for o in (1, -1) for i in OFFSETS])
    order_c = jnp.stack([column(i, 2) for i in OFFSETS] + bands)

    reduced = []
    basis_own = []
    basis_send = []
    for group in range(GROUPS):
        piece = own_half[:, group * part : (group + 1) * part]
        held = [piece] + [
            move(piece, by_core(along_x(-o), along_ring(-o))) for o in OFFSETS[1:]
        ]
        held = jnp.stack(held)
        ahead = move(held, by_core(along_ring(-1), along_x(-1)))
        behind = move(held, by_core(along_ring(1), along_x(1)))
        far_a = move(ahead[:2], by_core(along_ring(-1), along_x(-1)))
        far_b = move(behind[2:], by_core(along_ring(1), along_x(1)))
        (acc,) = project(order_a, grads, [held], None, False)
        (acc,) = project(order_b, grads, [ahead, behind], acc, False)
        sums = project(order_c, grads, [far_a, far_b], acc, True)
        basis_own.append(held)
        basis_send.append(jnp.stack([held[0], ahead[0], behind[0], far_a[0]]))
        total = sums[0]
        for dy in range(1, Y):
            got = move(sums[dy], along_y(OFFSETS[dy]))
            total = total + got.astype(jnp.float32)
        got = move(total[1].astype(jnp.bfloat16), other_half)
        reduced.append(total[0] + got.astype(jnp.float32))
    reduced = jnp.concatenate(reduced, axis=1)
    mine = lax.dynamic_slice(reduced, (c * owned, 0), (owned, half))
    theirs = lax.dynamic_slice(reduced, ((1 - c) * owned, 0), (owned, half))
    other = move(theirs, other_core)
    projected = jnp.where(
        c == 0,
        jnp.concatenate([mine, other], axis=1),
        jnp.concatenate([other, mine], axis=1),
    ).reshape(1, owned, rank_cols)
    new_first = beta_one * first_moment + (1.0 - beta_one) * projected
    new_second = beta_two * second_moment + (1.0 - beta_two) * projected * projected
    direction = new_first / bias_one / (jnp.sqrt(new_second / bias_two) + epsilon)
    direction = direction.astype(jnp.bfloat16).reshape(owned, rank_cols)

    basis_own = jnp.concatenate(basis_own, axis=2)
    basis_other = move(jnp.concatenate(basis_send, axis=2), other_core)
    basis = jnp.where(
        c == 0,
        jnp.concatenate([basis_own, basis_other], axis=2),
        jnp.concatenate([basis_other, basis_own], axis=2),
    )
    gathered = jnp.stack(
        [direction]
        + [
            move(direction, by_core(along_line(-o), along_x(-o)))
            for o in OFFSETS[1:]
        ]
    ).reshape(4 * owned, rank_cols)
    pieces = []
    for i, offset in enumerate(OFFSETS):
        value = lax.dot_general(
            gathered,
            basis[i],
            (((1,), (1,)), ((), ())),
            preferred_element_type=jnp.float32,
        ).astype(jnp.bfloat16)
        if offset:
            value = move(value, by_core(along_x(offset), along_line(offset)))
        pieces.append(value.reshape(4, owned, depth))
    result = jnp.zeros((X * ZL, owned, depth), jnp.bfloat16)
    for i, outer in enumerate(OFFSETS):
        for j, inner in enumerate(OFFSETS):
            result = lax.dynamic_update_slice(
                result, pieces[i][j : j + 1], (column(-outer, inner), 0, 0)
            )
    update = result.reshape(1, X * ZL * owned, depth)
    return (update, new_first, new_second)


def solution(mesh):
    in_specs = (
        P("dp", None, "fsdp", None),
        P("fsdp", None),
        P("dp", "fsdp", None),
        P("dp", "fsdp", None),
    )
    out_specs = (P("dp", None, "fsdp"), P("dp", "fsdp", None), P("dp", "fsdp", None))
    return jax.shard_map(
        per_device, mesh=mesh, in_specs=in_specs, out_specs=out_specs, check_vma=False
    )
```

```python
import functools

import jax
import jax.numpy as jnp
import numpy as np
from jax import lax
from jax.experimental import pallas as pl
from jax.experimental.pallas import tpu as pltpu
from jax.sharding import PartitionSpec as P

beta_one = 0.9
beta_two = 0.999
bias_one = 1.0 - 0.9**10
bias_two = 1.0 - 0.999**10
epsilon = 1e-08

ZH, Y, C, X, ZL = 2, 4, 2, 4, 4
AXES = ("dp", "fsdp")
OFFSETS = (0, 1, -1, 2)
GROUPS = 2


def linear(zh, y, c, x, zl):
    return (((zh * Y + y) * C + c) * X + x) * ZL + zl


def move(value, place):
    pairs = []
    for zh in range(ZH):
        for y in range(Y):
            for c in range(C):
                for x in range(X):
                    for zl in range(ZL):
                        target = place(zh, y, c, x, zl)
                        pairs.append((linear(zh, y, c, x, zl), linear(*target)))
    return lax.ppermute(value, AXES, pairs)


def along_x(step):
    return lambda zh, y, c, x, zl: (zh, y, c, (x + step) % X, zl)


def along_y(step):
    return lambda zh, y, c, x, zl: (zh, (y + step) % Y, c, x, zl)


def along_ring(step):
    def place(zh, y, c, x, zl):
        z = (zh * ZL + zl + step) % (ZH * ZL)
        return (z // ZL, y, c, x, z % ZL)

    return place


def along_line(step):
    return lambda zh, y, c, x, zl: (zh, y, c, x, (zl + step) % ZL)


def other_core(zh, y, c, x, zl):
    return (zh, y, 1 - c, x, zl)


def other_half(zh, y, c, x, zl):
    return (1 - zh, y, c, x, zl)


def by_core(first, second):
    def place(zh, y, c, x, zl):
        return (first if c == 0 else second)(zh, y, c, x, zl)

    return place


def block_at(c, x, zl, inner, outer):
    dx, dz = (inner, outer) if c == 0 else (outer, inner)
    return (x + dx) % X * ZL + (zl + dz) % ZL


def places_of(zh, y, c, x, zl):
    blocks = [block_at(c, x, zl, i, o) for o in OFFSETS for i in OFFSETS]
    rows = [block_at(c, x, zl, -i, o) for i in OFFSETS for o in OFFSETS]
    bands = [(y + o) % Y for o in OFFSETS]
    return blocks + bands + [zh, 1 - zh] + rows + [c]


BANDS = len(OFFSETS) ** 2
SLOTS = BANDS + Y
ROWS = SLOTS + ZH
CORE = ROWS + len(OFFSETS) ** 2


def all_places():
    return np.array(
        [
            places_of(zh, y, c, x, zl)
            for zh in range(ZH)
            for y in range(Y)
            for c in range(C)
            for x in range(X)
            for zl in range(ZL)
        ],
        np.int32,
    )


def project_kernel(outers, last, has_acc, places, *refs):
    grad, rest = refs[0], refs[1:]
    outs = rest[-(Y if last else 2) :]
    rest = rest[: -len(outs)]
    if has_acc:
        acc, rest = rest[-1], rest[:-1]
    pieces = [
        (OFFSETS.index(outer) * len(OFFSETS) + i, right, i)
        for outer, right in zip(outers, rest)
        for i in range(len(OFFSETS))
    ]
    depth, width = rest[0].shape[1:]
    band = grad.shape[1] // Y
    for dy in range(Y):
        row = places[BANDS + dy] if last else dy
        at = pl.ds(pl.multiple_of(row * band, 16), band)
        value = None
        for n, right, i in pieces:
            columns = pl.ds(pl.multiple_of(places[n] * depth, depth), depth)
            term = jnp.dot(
                grad[:, at, columns].reshape(ZH * band, depth),
                right[i],
                preferred_element_type=jnp.float32,
            )
            value = term if value is None else value + term
        value = value.reshape(ZH, band, width)
        if has_acc:
            value = value + acc[:, at, :]
        if last:
            for h in range(ZH):
                slot = places[SLOTS + h]
                outs[dy][slot] = value[h].astype(outs[dy].dtype)
        else:
            outs[0][:, at, :] = value
    if not last:
        outs[1][...] = value[0, : outs[1].shape[0], : outs[1].shape[1]]


def project(places, outers, grad, rights, acc, last):
    depth, width = rights[0].shape[1:]
    half_rows = grad.shape[1]
    count = sum(right.shape[0] for right in rights)
    whole = pl.BlockSpec(memory_space=pltpu.VMEM)
    operands = [grad, *rights] + ([] if acc is None else [acc])
    if last:
        shapes = [
            jax.ShapeDtypeStruct(
                (ZH, half_rows // Y, width), jnp.float32 if dy == 0 else jnp.bfloat16
            )
            for dy in range(Y)
        ]
    else:
        shapes = [
            jax.ShapeDtypeStruct((ZH, half_rows, width), jnp.float32),
            jax.ShapeDtypeStruct((8, 128), jnp.float32),
        ]
    return pl.pallas_call(
        functools.partial(project_kernel, outers, last, acc is not None),
        out_shape=shapes,
        in_specs=[pl.BlockSpec(memory_space=pltpu.SMEM)] + [whole] * len(operands),
        out_specs=[whole] * len(shapes),
        compiler_params=pltpu.CompilerParams(vmem_limit_bytes=14 * 1024 * 1024),
        cost_estimate=pl.CostEstimate(
            flops=2 * count * ZH * half_rows * depth * width,
            bytes_accessed=2 * count * depth * (2 * half_rows + width),
            transcendentals=0,
        ),
    )(places, *operands)


def stack_kernel(*refs):
    near, outs = refs[: len(OFFSETS)], refs[len(OFFSETS) + 2 :]
    for group, out in enumerate(outs):
        for i, piece in enumerate(near):
            out[i] = piece[group]


def stack_near(near, grad, places):
    groups, depth, width = near[0].shape
    whole = pl.BlockSpec(memory_space=pltpu.VMEM)
    return pl.pallas_call(
        stack_kernel,
        out_shape=[jax.ShapeDtypeStruct((len(near), depth, width), near[0].dtype)]
        * groups,
        in_specs=[whole] * len(near)
        + [pl.BlockSpec(memory_space=pltpu.HBM), pl.BlockSpec(memory_space=pltpu.SMEM)],
        out_specs=[whole] * groups,
        compiler_params=pltpu.CompilerParams(vmem_limit_bytes=5 * 1024 * 1024),
    )(*near, grad, places)


def add_kernel(first, second, out, slots, sems):
    band = slots.shape[2]
    per_half = out.shape[1] // band
    count = out.shape[0] * per_half

    def copies(n):
        at = (n // per_half, pl.ds((n % per_half) * band, band))
        return [
            pltpu.make_async_copy(
                ref.at[at], slots.at[side, n % 2], sems.at[side, n % 2]
            )
            for side, ref in enumerate((first, second))
        ]

    for copy in copies(0):
        copy.start()
    for n in range(count):
        if n + 1 < count:
            for copy in copies(n + 1):
                copy.start()
        for copy in copies(n):
            copy.wait()
        row = (n % per_half) * band

        def rows_on(i, carry):
            at = pl.ds(pl.multiple_of(i * 16, 16), 16)
            into = pl.ds(pl.multiple_of(row + i * 16, 16), 16)
            out[n // per_half, into, :] = slots[0, n % 2, at] + slots[1, n % 2, at]
            return carry

        lax.fori_loop(0, band // 16, rows_on, 0)


def add(first, second):
    halves, rows, width = first.shape
    band = rows // 4
    anywhere = pl.BlockSpec(memory_space=pltpu.HBM)
    return pl.pallas_call(
        add_kernel,
        out_shape=jax.ShapeDtypeStruct(first.shape, first.dtype),
        in_specs=[anywhere, anywhere],
        out_specs=pl.BlockSpec(memory_space=pltpu.VMEM),
        scratch_shapes=[
            pltpu.VMEM((2, 2, band, width), first.dtype),
            pltpu.SemaphoreType.DMA((2, 2)),
        ],
        compiler_params=pltpu.CompilerParams(vmem_limit_bytes=13 * 1024 * 1024),
        cost_estimate=pl.CostEstimate(
            flops=halves * rows * width,
            bytes_accessed=6 * halves * rows * width,
            transcendentals=0,
        ),
    )(first, second)


def pass_on(value, *after):
    main = pl.BlockSpec(memory_space=pltpu.HBM)
    return pl.pallas_call(
        lambda *refs: None,
        out_shape=jax.ShapeDtypeStruct(value.shape, value.dtype),
        in_specs=[main] + [pl.BlockSpec(memory_space=pl.ANY)] * len(after),
        out_specs=main,
        input_output_aliases={0: 0},
        compiler_params=pltpu.CompilerParams(vmem_limit_bytes=1024 * 1024),
    )(value, *after)


def collect_kernel(*refs):
    ins, out = refs[:-1], refs[-1]
    pieces, _, width = out.shape
    part = ins[0].shape[2]
    for n, ref in enumerate(ins):
        group, piece = n // pieces, n % pieces
        out[piece, :, group * part : (group + 1) * part] = ref[0]


def collect(groups):
    arrays = [array for group in groups for array in group]
    _, depth, part = arrays[0].shape
    pieces, width = len(groups[0]), part * len(groups)
    return pl.pallas_call(
        collect_kernel,
        grid=(1,),
        out_shape=jax.ShapeDtypeStruct((pieces, depth, width), arrays[0].dtype),
        in_specs=[pl.BlockSpec((1, depth, part), lambda i: (0, 0, 0))] * len(arrays),
        out_specs=pl.BlockSpec((pieces, depth, width), lambda i: (0, 0, 0)),
        compiler_params=pltpu.CompilerParams(vmem_limit_bytes=5 * 1024 * 1024),
    )(*arrays)


def split_kernel(groups, places, *refs):
    sums, mine, theirs = refs[:-2], refs[-2], refs[-1]
    owned = mine.shape[0]
    own = pl.ds(pl.multiple_of(places[CORE] * owned, 8), owned)
    other = pl.ds(pl.multiple_of((1 - places[CORE]) * owned, 8), owned)
    part = mine.shape[1] // groups
    for group in range(groups):
        kept, got = sums[2 * group : 2 * group + 2]
        at = slice(group * part, (group + 1) * part)
        mine[:, at] = kept[own, :] + got[own, :]
        theirs[:, at] = kept[other, :] + got[other, :]


def split(places, sums):
    groups = len(sums) // 2
    rows, part = sums[0].shape
    whole = pl.BlockSpec(memory_space=pltpu.VMEM)
    return pl.pallas_call(
        functools.partial(split_kernel, groups),
        out_shape=[jax.ShapeDtypeStruct((rows // C, part * groups), jnp.float32)] * 2,
        in_specs=[pl.BlockSpec(memory_space=pltpu.SMEM)] + [whole] * len(sums),
        out_specs=[whole] * 2,
        compiler_params=pltpu.CompilerParams(vmem_limit_bytes=5 * 1024 * 1024),
    )(places, *sums)


def adam_kernel(places, mine, other, first, second, new_first, new_second, direction):
    half = mine.shape[1]
    is_first = places[CORE] == 0
    own, far = mine[...], other[...]
    for n in range(C):
        at = slice(n * half, (n + 1) * half)
        value = jnp.where(is_first, far, own) if n else jnp.where(is_first, own, far)
        moment = beta_one * first[0, :, at] + (1.0 - beta_one) * value
        square = beta_two * second[0, :, at] + (1.0 - beta_two) * value * value
        new_first[0, :, at] = moment
        new_second[0, :, at] = square
    for n in range(C):
        step = []
        for m in (n, 1 - n):
            at = slice(m * half, (m + 1) * half)
            root = jnp.sqrt(new_second[0, :, at] / bias_two) + epsilon
            step.append(new_first[0, :, at] / bias_one / root)
        value = jnp.where(is_first, step[0], step[1])
        direction[:, n * half : (n + 1) * half] = value.astype(direction.dtype)


def adam(places, mine, other, first, second):
    whole = pl.BlockSpec(memory_space=pltpu.VMEM)
    return pl.pallas_call(
        adam_kernel,
        out_shape=[
            jax.ShapeDtypeStruct(first.shape, jnp.float32),
            jax.ShapeDtypeStruct(first.shape, jnp.float32),
            jax.ShapeDtypeStruct(first.shape[1:], jnp.bfloat16),
        ],
        in_specs=[pl.BlockSpec(memory_space=pltpu.SMEM)] + [whole] * 4,
        out_specs=[whole] * 3,
        compiler_params=pltpu.CompilerParams(vmem_limit_bytes=5 * 1024 * 1024),
    )(places, mine, other, first, second)


def place_kernel(places, *refs):
    pieces, out = refs[:-1], refs[-1]
    for i, piece in enumerate(pieces):
        for j in range(len(OFFSETS)):
            out[places[ROWS + i * len(OFFSETS) + j]] = piece[j]


def place_rows(places, pieces):
    count, owned, depth = pieces[0].shape
    whole = pl.BlockSpec(memory_space=pltpu.VMEM)
    return pl.pallas_call(
        place_kernel,
        out_shape=jax.ShapeDtypeStruct((count * len(pieces), owned, depth), jnp.bfloat16),
        in_specs=[pl.BlockSpec(memory_space=pltpu.SMEM)] + [whole] * len(pieces),
        out_specs=whole,
        compiler_params=pltpu.CompilerParams(vmem_limit_bytes=5 * 1024 * 1024),
    )(places, *pieces)


def per_device(gradient, projector, first_moment, second_moment):
    blocks = gradient.shape[1]
    owned = gradient.shape[2]
    width = gradient.shape[3]
    depth, rank_cols = projector.shape
    half = rank_cols // 2
    part = half // GROUPS
    rows = blocks * owned
    dp = lax.axis_index("dp")
    fsdp = lax.axis_index("fsdp")
    places = lax.dynamic_index_in_dim(
        jnp.asarray(all_places()), dp * (X * ZL) + fsdp, 0, keepdims=False
    )
    c = dp % C

    own_grad = gradient.reshape(ZH, rows // ZH, width)
    other_grad = move(own_grad, other_core)
    both = add(own_grad, other_grad)
    own_half = lax.dynamic_slice(projector, (0, c * half), (depth, half))
    own_half = jnp.stack(
        [own_half[:, g * part : (g + 1) * part] for g in range(GROUPS)]
    )
    near = [own_half] + [
        move(own_half, by_core(along_x(-o), along_ring(-o))) for o in OFFSETS[1:]
    ]

    reduced = []
    stacks = stack_near(near, other_grad, places)
    ahead = [move(held, by_core(along_ring(-1), along_x(-1))) for held in stacks]
    behind = [move(held, by_core(along_ring(1), along_x(1))) for held in stacks]
    accs, done = zip(
        *[project(places, (0,), both, [held], None, False) for held in stacks]
    )
    ahead[0] = pass_on(ahead[0], *done)
    behind[1] = pass_on(behind[1], *done)
    far = [
        move(ahead[0], by_core(along_ring(-1), along_x(-1))),
        move(behind[1], by_core(along_ring(1), along_x(1))),
    ]
    for group in range(GROUPS):
        acc, _ = project(
            places, (1, -1), both, [ahead[group], behind[group]], accs[group], False
        )
        sums = project(places, (2,), both, [far[group]], acc, True)
        total = sums[0]
        for dy in range(1, Y):
            got = move(sums[dy], along_y(OFFSETS[dy]))
            total = total + got.astype(jnp.float32)
        got = move(total[1].astype(jnp.bfloat16), other_half)
        reduced += [total[0], got.astype(jnp.float32)]
    mine, theirs = split(places, reduced)
    other = move(theirs, other_core)
    new_first, new_second, direction = adam(
        places, mine, other, first_moment, second_moment
    )
    basis_other = move(collect(list(zip(stacks, ahead, behind, far))), other_core)
    basis = jnp.concatenate([*stacks, basis_other], axis=2)
    gathered = jnp.stack(
        [direction]
        + [
            move(direction, by_core(along_line(-o), along_x(-o)))
            for o in OFFSETS[1:]
        ]
    ).reshape(4 * owned, rank_cols)
    pieces = []
    for i, offset in enumerate(OFFSETS):
        value = lax.dot_general(
            gathered,
            basis[i],
            (((1,), (1,)), ((), ())),
            preferred_element_type=jnp.float32,
        ).astype(jnp.bfloat16)
        if offset:
            value = move(value, by_core(along_x(offset), along_line(offset)))
        pieces.append(value.reshape(4, owned, depth))
    result = place_rows(places, pieces)
    update = result.reshape(1, X * ZL * owned, depth)
    return (update, new_first, new_second)


def solution(mesh):
    in_specs = (
        P("dp", None, "fsdp", None),
        P("fsdp", None),
        P("dp", "fsdp", None),
        P("dp", "fsdp", None),
    )
    out_specs = (P("dp", None, "fsdp"), P("dp", "fsdp", None), P("dp", "fsdp", None))
    return jax.shard_map(
        per_device, mesh=mesh, in_specs=in_specs, out_specs=out_specs, check_vma=False
    )
```

```python
import functools

import jax
import jax.numpy as jnp
import numpy as np
from jax import lax
from jax.experimental import pallas as pl
from jax.experimental.pallas import tpu as pltpu
from jax.sharding import PartitionSpec as P

beta_one = 0.9
beta_two = 0.999
bias_one = 1.0 - 0.9**10
bias_two = 1.0 - 0.999**10
epsilon = 1e-08

ZH, Y, C, X, ZL = 2, 4, 2, 4, 4
AXES = ("dp", "fsdp")
OFFSETS = (0, 1, -1, 2)
GROUPS = 2


def linear(zh, y, c, x, zl):
    return (((zh * Y + y) * C + c) * X + x) * ZL + zl


def move(value, place):
    pairs = []
    for zh in range(ZH):
        for y in range(Y):
            for c in range(C):
                for x in range(X):
                    for zl in range(ZL):
                        target = place(zh, y, c, x, zl)
                        pairs.append((linear(zh, y, c, x, zl), linear(*target)))
    return lax.ppermute(value, AXES, pairs)


def along_x(step):
    return lambda zh, y, c, x, zl: (zh, y, c, (x + step) % X, zl)


def along_y(step):
    return lambda zh, y, c, x, zl: (zh, (y + step) % Y, c, x, zl)


def along_ring(step):
    def place(zh, y, c, x, zl):
        z = (zh * ZL + zl + step) % (ZH * ZL)
        return (z // ZL, y, c, x, z % ZL)

    return place


def two_along_ring(zh, y, c, x, zl):
    return along_ring(2 if zl % 2 else -2)(zh, y, c, x, zl)


def along_line(step):
    return lambda zh, y, c, x, zl: (zh, y, c, x, (zl + step) % ZL)


def other_core(zh, y, c, x, zl):
    return (zh, y, 1 - c, x, zl)


def other_half(zh, y, c, x, zl):
    return (1 - zh, y, c, x, zl)


def by_core(first, second):
    def place(zh, y, c, x, zl):
        return (first if c == 0 else second)(zh, y, c, x, zl)

    return place


def block_at(c, x, zl, inner, outer):
    dx, dz = (inner, outer) if c == 0 else (outer, inner)
    return (x + dx) % X * ZL + (zl + dz) % ZL


def places_of(zh, y, c, x, zl):
    blocks = [block_at(c, x, zl, i, o) for o in OFFSETS for i in OFFSETS]
    rows = [block_at(c, x, zl, -i, o) for i in OFFSETS for o in OFFSETS]
    bands = [(y + o) % Y for o in OFFSETS]
    return blocks + bands + [zh, 1 - zh] + rows + [c]


BANDS = len(OFFSETS) ** 2
SLOTS = BANDS + Y
ROWS = SLOTS + ZH
CORE = ROWS + len(OFFSETS) ** 2


def all_places():
    return np.array(
        [
            places_of(zh, y, c, x, zl)
            for zh in range(ZH)
            for y in range(Y)
            for c in range(C)
            for x in range(X)
            for zl in range(ZL)
        ],
        np.int32,
    )


def project_kernel(outers, last, has_acc, after, places, *refs):
    grad, rest = refs[0], refs[1:]
    outs = rest[-(Y if last else 2) :]
    rest = rest[: len(rest) - len(outs) - after]
    if has_acc:
        acc, rest = rest[-1], rest[:-1]
    pieces = [
        (OFFSETS.index(outer) * len(OFFSETS) + i, right, i)
        for outer, right in zip(outers, rest)
        for i in range(len(OFFSETS))
    ]
    depth, width = rest[0].shape[1:]
    band = grad.shape[1] // Y
    for dy in range(Y):
        row = places[BANDS + dy] if last else dy
        at = pl.ds(pl.multiple_of(row * band, 16), band)
        value = None
        for n, right, i in pieces:
            columns = pl.ds(pl.multiple_of(places[n] * depth, depth), depth)
            term = jnp.dot(
                grad[:, at, columns].reshape(ZH * band, depth),
                right[i],
                preferred_element_type=jnp.float32,
            )
            value = term if value is None else value + term
        value = value.reshape(ZH, band, width)
        if has_acc:
            value = value + acc[:, at, :]
        if last:
            for h in range(ZH):
                slot = places[SLOTS + h]
                outs[dy][slot] = value[h].astype(outs[dy].dtype)
        else:
            outs[0][:, at, :] = value
    if not last:
        outs[1][...] = value[0, : outs[1].shape[0], : outs[1].shape[1]]


def project(places, outers, grad, rights, acc, last, after=()):
    depth, width = rights[0].shape[1:]
    half_rows = grad.shape[1]
    count = sum(right.shape[0] for right in rights)
    whole = pl.BlockSpec(memory_space=pltpu.VMEM)
    operands = [grad, *rights] + ([] if acc is None else [acc]) + list(after)
    if last:
        shapes = [
            jax.ShapeDtypeStruct(
                (ZH, half_rows // Y, width), jnp.float32 if dy == 0 else jnp.bfloat16
            )
            for dy in range(Y)
        ]
    else:
        shapes = [
            jax.ShapeDtypeStruct((ZH, half_rows, width), jnp.float32),
            jax.ShapeDtypeStruct((8, 128), jnp.float32),
        ]
    return pl.pallas_call(
        functools.partial(
            project_kernel, outers, last, acc is not None, len(after)
        ),
        out_shape=shapes,
        in_specs=[pl.BlockSpec(memory_space=pltpu.SMEM)] + [whole] * len(operands),
        out_specs=[whole] * len(shapes),
        compiler_params=pltpu.CompilerParams(vmem_limit_bytes=14 * 1024 * 1024),
        cost_estimate=pl.CostEstimate(
            flops=2 * count * ZH * half_rows * depth * width,
            bytes_accessed=2 * count * depth * (2 * half_rows + width),
            transcendentals=0,
        ),
    )(places, *operands)


def stack_kernel(*refs):
    near, outs = refs[: len(OFFSETS)], refs[len(OFFSETS) + 2 :]
    for group, out in enumerate(outs):
        for i, piece in enumerate(near):
            out[i] = piece[group]


def stack_near(near, grad, places):
    groups, depth, width = near[0].shape
    whole = pl.BlockSpec(memory_space=pltpu.VMEM)
    return pl.pallas_call(
        stack_kernel,
        out_shape=[jax.ShapeDtypeStruct((len(near), depth, width), near[0].dtype)]
        * groups,
        in_specs=[whole] * len(near)
        + [pl.BlockSpec(memory_space=pltpu.HBM), pl.BlockSpec(memory_space=pltpu.SMEM)],
        out_specs=[whole] * groups,
        compiler_params=pltpu.CompilerParams(vmem_limit_bytes=5 * 1024 * 1024),
    )(*near, grad, places)


def add_kernel(first, second, out, slots, sems):
    band = slots.shape[1]
    per_half = out.shape[1] // band
    count = out.shape[0] * per_half
    depth = slots.shape[0]

    def copy(n):
        at = (n // per_half, pl.ds((n % per_half) * band, band))
        return pltpu.make_async_copy(
            second.at[at], slots.at[n % depth], sems.at[n % depth]
        )

    for n in range(depth - 1):
        copy(n).start()
    for n in range(count):
        if n + depth - 1 < count:
            copy(n + depth - 1).start()
        copy(n).wait()
        half, row = n // per_half, (n % per_half) * band

        def rows_on(i, carry):
            at = pl.ds(pl.multiple_of(i * 16, 16), 16)
            into = pl.ds(pl.multiple_of(row + i * 16, 16), 16)
            out[half, into, :] = first[half, into, :] + slots[n % depth, at]
            return carry

        lax.fori_loop(0, band // 16, rows_on, 0)


def add(first, second):
    halves, rows, width = first.shape
    band = rows // 4
    whole = pl.BlockSpec(memory_space=pltpu.VMEM)
    return pl.pallas_call(
        add_kernel,
        out_shape=jax.ShapeDtypeStruct(first.shape, first.dtype),
        in_specs=[whole, pl.BlockSpec(memory_space=pltpu.HBM)],
        out_specs=whole,
        scratch_shapes=[
            pltpu.VMEM((3, band, width), first.dtype),
            pltpu.SemaphoreType.DMA((3,)),
        ],
        compiler_params=pltpu.CompilerParams(vmem_limit_bytes=19 * 1024 * 1024),
        cost_estimate=pl.CostEstimate(
            flops=halves * rows * width,
            bytes_accessed=6 * halves * rows * width,
            transcendentals=0,
        ),
    )(first, second)


def pass_on(value, *after):
    main = pl.BlockSpec(memory_space=pltpu.HBM)
    return pl.pallas_call(
        lambda *refs: None,
        out_shape=jax.ShapeDtypeStruct(value.shape, value.dtype),
        in_specs=[main] + [pl.BlockSpec(memory_space=pl.ANY)] * len(after),
        out_specs=main,
        input_output_aliases={0: 0},
        compiler_params=pltpu.CompilerParams(vmem_limit_bytes=1024 * 1024),
    )(value, *after)


def collect_kernel(pieces, groups, *refs):
    ins, out = refs[: pieces * groups], refs[-1]
    part = ins[0].shape[2]
    for n, ref in enumerate(ins):
        group, piece = n // pieces, n % pieces
        out[piece, :, group * part : (group + 1) * part] = ref[0]


def collect(groups, *after):
    arrays = [array for group in groups for array in group]
    _, depth, part = arrays[0].shape
    pieces, width = len(groups[0]), part * len(groups)
    first = pl.BlockSpec((1, depth, part), lambda i: (0, 0, 0))
    one = [pl.BlockSpec((8, 128), lambda i: (0, 0))] * len(after)
    return pl.pallas_call(
        functools.partial(collect_kernel, pieces, len(groups)),
        grid=(1,),
        out_shape=jax.ShapeDtypeStruct((pieces, depth, width), arrays[0].dtype),
        in_specs=[first] * len(arrays) + one,
        out_specs=pl.BlockSpec((pieces, depth, width), lambda i: (0, 0, 0)),
        compiler_params=pltpu.CompilerParams(vmem_limit_bytes=5 * 1024 * 1024),
    )(*arrays, *after)


def split_kernel(groups, places, *refs):
    sums, mine, theirs = refs[:-2], refs[-2], refs[-1]
    owned = mine.shape[0]
    own = pl.ds(pl.multiple_of(places[CORE] * owned, 8), owned)
    other = pl.ds(pl.multiple_of((1 - places[CORE]) * owned, 8), owned)
    part = mine.shape[1] // groups
    for group in range(groups):
        kept, got = sums[2 * group : 2 * group + 2]
        at = slice(group * part, (group + 1) * part)
        mine[:, at] = kept[own, :] + got[own, :]
        theirs[:, at] = kept[other, :] + got[other, :]


def split(places, sums):
    groups = len(sums) // 2
    rows, part = sums[0].shape
    whole = pl.BlockSpec(memory_space=pltpu.VMEM)
    return pl.pallas_call(
        functools.partial(split_kernel, groups),
        out_shape=[jax.ShapeDtypeStruct((rows // C, part * groups), jnp.float32)] * 2,
        in_specs=[pl.BlockSpec(memory_space=pltpu.SMEM)] + [whole] * len(sums),
        out_specs=[whole] * 2,
        compiler_params=pltpu.CompilerParams(vmem_limit_bytes=5 * 1024 * 1024),
    )(places, *sums)


def adam_kernel(places, mine, other, first, second, new_first, new_second, direction):
    half = mine.shape[1]
    is_first = places[CORE] == 0
    own, far = mine[...], other[...]
    for n in range(C):
        at = slice(n * half, (n + 1) * half)
        value = jnp.where(is_first, far, own) if n else jnp.where(is_first, own, far)
        moment = beta_one * first[0, :, at] + (1.0 - beta_one) * value
        square = beta_two * second[0, :, at] + (1.0 - beta_two) * value * value
        new_first[0, :, at] = moment
        new_second[0, :, at] = square
    for n in range(C):
        step = []
        for m in (n, 1 - n):
            at = slice(m * half, (m + 1) * half)
            root = jnp.sqrt(new_second[0, :, at] / bias_two) + epsilon
            step.append(new_first[0, :, at] / bias_one / root)
        value = jnp.where(is_first, step[0], step[1])
        direction[:, n * half : (n + 1) * half] = value.astype(direction.dtype)


def adam(places, mine, other, first, second):
    whole = pl.BlockSpec(memory_space=pltpu.VMEM)
    return pl.pallas_call(
        adam_kernel,
        out_shape=[
            jax.ShapeDtypeStruct(first.shape, jnp.float32),
            jax.ShapeDtypeStruct(first.shape, jnp.float32),
            jax.ShapeDtypeStruct(first.shape[1:], jnp.bfloat16),
        ],
        in_specs=[pl.BlockSpec(memory_space=pltpu.SMEM)] + [whole] * 4,
        out_specs=[whole] * 3,
        compiler_params=pltpu.CompilerParams(vmem_limit_bytes=5 * 1024 * 1024),
    )(places, mine, other, first, second)


def place_kernel(places, *refs):
    pieces, out = refs[:-1], refs[-1]
    for i, piece in enumerate(pieces):
        for j in range(len(OFFSETS)):
            out[places[ROWS + i * len(OFFSETS) + j]] = piece[j]


def place_rows(places, pieces):
    count, owned, depth = pieces[0].shape
    whole = pl.BlockSpec(memory_space=pltpu.VMEM)
    return pl.pallas_call(
        place_kernel,
        out_shape=jax.ShapeDtypeStruct((count * len(pieces), owned, depth), jnp.bfloat16),
        in_specs=[pl.BlockSpec(memory_space=pltpu.SMEM)] + [whole] * len(pieces),
        out_specs=whole,
        compiler_params=pltpu.CompilerParams(vmem_limit_bytes=5 * 1024 * 1024),
    )(places, *pieces)


def per_device(gradient, projector, first_moment, second_moment):
    blocks = gradient.shape[1]
    owned = gradient.shape[2]
    width = gradient.shape[3]
    depth, rank_cols = projector.shape
    half = rank_cols // 2
    part = half // GROUPS
    rows = blocks * owned
    dp = lax.axis_index("dp")
    fsdp = lax.axis_index("fsdp")
    places = lax.dynamic_index_in_dim(
        jnp.asarray(all_places()), dp * (X * ZL) + fsdp, 0, keepdims=False
    )
    c = dp % C

    own_grad = gradient.reshape(ZH, rows // ZH, width)
    other_grad = move(own_grad, other_core)
    both = add(own_grad, other_grad)
    own_half = lax.dynamic_slice(projector, (0, c * half), (depth, half))
    own_half = jnp.stack(
        [own_half[:, g * part : (g + 1) * part] for g in range(GROUPS)]
    )
    near = [
        own_half,
        move(own_half, by_core(along_x(-1), along_ring(-1))),
        move(own_half, by_core(along_x(1), along_ring(1))),
        move(own_half, by_core(along_x(2), two_along_ring)),
    ]

    reduced = []
    stacks = stack_near(near, other_grad, places)
    ahead = [move(held, by_core(along_ring(-1), along_x(-1))) for held in stacks]
    behind = [move(held, by_core(along_ring(1), along_x(1))) for held in stacks]
    accs, done = zip(
        *[project(places, (0,), both, [held], None, False) for held in stacks]
    )
    ahead[0] = pass_on(ahead[0], *done)
    behind[1] = pass_on(behind[1], *done)
    far = [
        move(ahead[0], by_core(along_ring(-1), along_x(-1))),
        move(behind[1], by_core(along_ring(1), along_x(1))),
    ]
    near_two = [ahead[0], behind[0]]
    acc0, _ = project(places, (1, -1), both, near_two, accs[0], False)
    acc1, token = project(places, (-1,), both, [behind[1]], accs[1], False)
    sums0 = project(places, (2,), both, [far[0]], acc0, True, (token,))
    sums1 = project(
        places, (1, 2), both, [ahead[1], far[1]], acc1, True, (sums0[1],)
    )
    for sums in (sums0, sums1):
        total = sums[0]
        for dy in range(1, Y):
            got = move(sums[dy], along_y(OFFSETS[dy]))
            total = total + got.astype(jnp.float32)
        got = move(total[1].astype(jnp.bfloat16), other_half)
        reduced += [total[0], got.astype(jnp.float32)]
    mine, theirs = split(places, reduced)
    other = move(theirs, other_core)
    new_first, new_second, direction = adam(
        places, mine, other, first_moment, second_moment
    )
    basis_other = move(
        collect(list(zip(stacks, ahead, behind, far))), other_core
    )
    basis = jnp.concatenate([*stacks, basis_other], axis=2)
    gathered = jnp.stack(
        [direction]
        + [
            move(direction, by_core(along_line(-o), along_x(-o)))
            for o in OFFSETS[1:]
        ]
    ).reshape(4 * owned, rank_cols)
    pieces = []
    for i, offset in enumerate(OFFSETS):
        value = lax.dot_general(
            gathered,
            basis[i],
            (((1,), (1,)), ((), ())),
            preferred_element_type=jnp.float32,
        ).astype(jnp.bfloat16)
        if offset:
            value = move(value, by_core(along_x(offset), along_line(offset)))
        pieces.append(value.reshape(4, owned, depth))
    result = place_rows(places, pieces)
    update = result.reshape(1, X * ZL * owned, depth)
    return (update, new_first, new_second)


def solution(mesh):
    in_specs = (
        P("dp", None, "fsdp", None),
        P("fsdp", None),
        P("dp", "fsdp", None),
        P("dp", "fsdp", None),
    )
    out_specs = (P("dp", None, "fsdp"), P("dp", "fsdp", None), P("dp", "fsdp", None))
    return jax.shard_map(
        per_device, mesh=mesh, in_specs=in_specs, out_specs=out_specs, check_vma=False
    )
```

```python
import functools

import jax
import jax.numpy as jnp
import numpy as np
from jax import lax
from jax.experimental import pallas as pl
from jax.experimental.pallas import tpu as pltpu
from jax.sharding import PartitionSpec as P

beta_one = 0.9
beta_two = 0.999
bias_one = 1.0 - 0.9**10
bias_two = 1.0 - 0.999**10
epsilon = 1e-08

ZH, Y, C, X, ZL = 2, 4, 2, 4, 4
AXES = ("dp", "fsdp")
OFFSETS = (0, 1, -1, 2)
GROUPS = 2


def linear(zh, y, c, x, zl):
    return (((zh * Y + y) * C + c) * X + x) * ZL + zl


def move(value, place):
    pairs = []
    for zh in range(ZH):
        for y in range(Y):
            for c in range(C):
                for x in range(X):
                    for zl in range(ZL):
                        target = place(zh, y, c, x, zl)
                        pairs.append((linear(zh, y, c, x, zl), linear(*target)))
    return lax.ppermute(value, AXES, pairs)


def along_x(step):
    return lambda zh, y, c, x, zl: (zh, y, c, (x + step) % X, zl)


def along_y(step):
    return lambda zh, y, c, x, zl: (zh, (y + step) % Y, c, x, zl)


def along_ring(step):
    def place(zh, y, c, x, zl):
        z = (zh * ZL + zl + step) % (ZH * ZL)
        return (z // ZL, y, c, x, z % ZL)

    return place


def two_along_ring(zh, y, c, x, zl):
    return along_ring(2 if zl % 2 else -2)(zh, y, c, x, zl)


def along_line(step):
    return lambda zh, y, c, x, zl: (zh, y, c, x, (zl + step) % ZL)


def other_core(zh, y, c, x, zl):
    return (zh, y, 1 - c, x, zl)


def other_half(zh, y, c, x, zl):
    return (1 - zh, y, c, x, zl)


def by_core(first, second):
    def place(zh, y, c, x, zl):
        return (first if c == 0 else second)(zh, y, c, x, zl)

    return place


def block_at(c, x, zl, inner, outer):
    dx, dz = (inner, outer) if c == 0 else (outer, inner)
    return (x + dx) % X * ZL + (zl + dz) % ZL


def places_of(zh, y, c, x, zl):
    blocks = [block_at(c, x, zl, i, o) for o in OFFSETS for i in OFFSETS]
    rows = [block_at(c, x, zl, -i, o) for i in OFFSETS for o in OFFSETS]
    bands = [(y + o) % Y for o in OFFSETS]
    return blocks + bands + [zh, 1 - zh] + rows + [c]


BANDS = len(OFFSETS) ** 2
SLOTS = BANDS + Y
ROWS = SLOTS + ZH
CORE = ROWS + len(OFFSETS) ** 2


def all_places():
    return np.array(
        [
            places_of(zh, y, c, x, zl)
            for zh in range(ZH)
            for y in range(Y)
            for c in range(C)
            for x in range(X)
            for zl in range(ZL)
        ],
        np.int32,
    )


def project_kernel(outers, last, has_acc, after, places, *refs):
    grad, rest = refs[0], refs[1:]
    outs = rest[-(Y if last else 2) :]
    rest = rest[: len(rest) - len(outs) - after]
    if has_acc:
        acc, rest = rest[-1], rest[:-1]
    pieces = [
        (OFFSETS.index(outer) * len(OFFSETS) + i, right, i)
        for outer, right in zip(outers, rest)
        for i in range(len(OFFSETS))
    ]
    depth, width = rest[0].shape[1:]
    band = grad.shape[1] // Y
    for dy in range(Y):
        row = places[BANDS + dy] if last else dy
        at = pl.ds(pl.multiple_of(row * band, 16), band)
        value = None
        for n, right, i in pieces:
            columns = pl.ds(pl.multiple_of(places[n] * depth, depth), depth)
            term = jnp.dot(
                grad[:, at, columns].reshape(ZH * band, depth),
                right[i],
                preferred_element_type=jnp.float32,
            )
            value = term if value is None else value + term
        value = value.reshape(ZH, band, width)
        if has_acc:
            value = value + acc[:, at, :]
        if last:
            for h in range(ZH):
                slot = places[SLOTS + h]
                outs[dy][slot] = value[h].astype(outs[dy].dtype)
        else:
            outs[0][:, at, :] = value
    if not last:
        outs[1][...] = value[0, : outs[1].shape[0], : outs[1].shape[1]]


def project(places, outers, grad, rights, acc, last, after=()):
    depth, width = rights[0].shape[1:]
    half_rows = grad.shape[1]
    count = sum(right.shape[0] for right in rights)
    whole = pl.BlockSpec(memory_space=pltpu.VMEM)
    operands = [grad, *rights] + ([] if acc is None else [acc]) + list(after)
    if last:
        shapes = [
            jax.ShapeDtypeStruct(
                (ZH, half_rows // Y, width), jnp.float32 if dy == 0 else jnp.bfloat16
            )
            for dy in range(Y)
        ]
    else:
        shapes = [
            jax.ShapeDtypeStruct((ZH, half_rows, width), jnp.float32),
            jax.ShapeDtypeStruct((8, 128), jnp.float32),
        ]
    return pl.pallas_call(
        functools.partial(
            project_kernel, outers, last, acc is not None, len(after)
        ),
        out_shape=shapes,
        in_specs=[pl.BlockSpec(memory_space=pltpu.SMEM)] + [whole] * len(operands),
        out_specs=[whole] * len(shapes),
        compiler_params=pltpu.CompilerParams(vmem_limit_bytes=14 * 1024 * 1024),
        cost_estimate=pl.CostEstimate(
            flops=2 * count * ZH * half_rows * depth * width,
            bytes_accessed=2 * count * depth * (2 * half_rows + width),
            transcendentals=0,
        ),
    )(places, *operands)


def stack_kernel(*refs):
    near, outs = refs[: len(OFFSETS)], refs[len(OFFSETS) + 2 :]
    for group, out in enumerate(outs):
        for i, piece in enumerate(near):
            out[i] = piece[group]


def stack_near(near, grad, places):
    groups, depth, width = near[0].shape
    whole = pl.BlockSpec(memory_space=pltpu.VMEM)
    return pl.pallas_call(
        stack_kernel,
        out_shape=[jax.ShapeDtypeStruct((len(near), depth, width), near[0].dtype)]
        * groups,
        in_specs=[whole] * len(near)
        + [pl.BlockSpec(memory_space=pltpu.HBM), pl.BlockSpec(memory_space=pltpu.SMEM)],
        out_specs=[whole] * groups,
        compiler_params=pltpu.CompilerParams(vmem_limit_bytes=5 * 1024 * 1024),
    )(*near, grad, places)


def add_kernel(first, second, out, slots, sems):
    band = slots.shape[1]
    per_half = out.shape[1] // band
    count = out.shape[0] * per_half
    depth = slots.shape[0]

    def copy(n):
        at = (n // per_half, pl.ds((n % per_half) * band, band))
        return pltpu.make_async_copy(
            second.at[at], slots.at[n % depth], sems.at[n % depth]
        )

    for n in range(depth - 1):
        copy(n).start()
    for n in range(count):
        if n + depth - 1 < count:
            copy(n + depth - 1).start()
        copy(n).wait()
        half, row = n // per_half, (n % per_half) * band

        def rows_on(i, carry):
            at = pl.ds(pl.multiple_of(i * 16, 16), 16)
            into = pl.ds(pl.multiple_of(row + i * 16, 16), 16)
            out[half, into, :] = first[half, into, :] + slots[n % depth, at]
            return carry

        lax.fori_loop(0, band // 16, rows_on, 0)


def add(first, second):
    halves, rows, width = first.shape
    band = rows // 4
    whole = pl.BlockSpec(memory_space=pltpu.VMEM)
    return pl.pallas_call(
        add_kernel,
        out_shape=jax.ShapeDtypeStruct(first.shape, first.dtype),
        in_specs=[whole, pl.BlockSpec(memory_space=pltpu.HBM)],
        out_specs=whole,
        scratch_shapes=[
            pltpu.VMEM((3, band, width), first.dtype),
            pltpu.SemaphoreType.DMA((3,)),
        ],
        compiler_params=pltpu.CompilerParams(vmem_limit_bytes=19 * 1024 * 1024),
        cost_estimate=pl.CostEstimate(
            flops=halves * rows * width,
            bytes_accessed=6 * halves * rows * width,
            transcendentals=0,
        ),
    )(first, second)


def pass_on(value, *after):
    main = pl.BlockSpec(memory_space=pltpu.HBM)
    return pl.pallas_call(
        lambda *refs: None,
        out_shape=jax.ShapeDtypeStruct(value.shape, value.dtype),
        in_specs=[main] + [pl.BlockSpec(memory_space=pl.ANY)] * len(after),
        out_specs=main,
        input_output_aliases={0: 0},
        compiler_params=pltpu.CompilerParams(vmem_limit_bytes=1024 * 1024),
    )(value, *after)


def collect_kernel(pieces, groups, *refs):
    ins, out = refs[: pieces * groups], refs[-1]
    part = ins[0].shape[2]
    for n, ref in enumerate(ins):
        group, piece = n // pieces, n % pieces
        out[piece, :, group * part : (group + 1) * part] = ref[0]


def collect(groups, *after):
    arrays = [array for group in groups for array in group]
    _, depth, part = arrays[0].shape
    pieces, width = len(groups[0]), part * len(groups)
    first = pl.BlockSpec((1, depth, part), lambda i: (0, 0, 0))
    one = [pl.BlockSpec((8, 128), lambda i: (0, 0))] * len(after)
    return pl.pallas_call(
        functools.partial(collect_kernel, pieces, len(groups)),
        grid=(1,),
        out_shape=jax.ShapeDtypeStruct((pieces, depth, width), arrays[0].dtype),
        in_specs=[first] * len(arrays) + one,
        out_specs=pl.BlockSpec((pieces, depth, width), lambda i: (0, 0, 0)),
        compiler_params=pltpu.CompilerParams(vmem_limit_bytes=5 * 1024 * 1024),
    )(*arrays, *after)


def split_kernel(groups, places, *refs):
    sums, mine, theirs = refs[:-2], refs[-2], refs[-1]
    owned = mine.shape[0]
    own = pl.ds(pl.multiple_of(places[CORE] * owned, 8), owned)
    other = pl.ds(pl.multiple_of((1 - places[CORE]) * owned, 8), owned)
    part = mine.shape[1] // groups
    for group in range(groups):
        kept, got = sums[2 * group : 2 * group + 2]
        at = slice(group * part, (group + 1) * part)
        mine[:, at] = kept[own, :] + got[own, :]
        theirs[:, at] = kept[other, :] + got[other, :]


def split(places, sums):
    groups = len(sums) // 2
    rows, part = sums[0].shape
    whole = pl.BlockSpec(memory_space=pltpu.VMEM)
    return pl.pallas_call(
        functools.partial(split_kernel, groups),
        out_shape=[jax.ShapeDtypeStruct((rows // C, part * groups), jnp.float32)] * 2,
        in_specs=[pl.BlockSpec(memory_space=pltpu.SMEM)] + [whole] * len(sums),
        out_specs=[whole] * 2,
        compiler_params=pltpu.CompilerParams(vmem_limit_bytes=5 * 1024 * 1024),
    )(places, *sums)


def halves(places, array, n):
    half = array.shape[2] // C
    parts = [array[0, :, m * half : (m + 1) * half] for m in (n, 1 - n)]
    return jnp.where(places[CORE] == 0, parts[0], parts[1])


def first_of(moment, value):
    return beta_one * moment + (1.0 - beta_one) * value


def second_of(moment, value):
    return beta_two * moment + (1.0 - beta_two) * value * value


def direction_kernel(places, mine, other, first, second, out):
    half = mine.shape[1]
    for n, ref in enumerate((mine, other)):
        value = ref[...]
        moment = first_of(halves(places, first, n), value)
        square = second_of(halves(places, second, n), value)
        step = moment / bias_one / (jnp.sqrt(square / bias_two) + epsilon)
        out[:, n * half : (n + 1) * half] = step.astype(out.dtype)


def moments_kernel(places, mine, other, first, second, after, new_first, new_second):
    half = mine.shape[1]
    is_first = places[CORE] == 0
    own, far = mine[...], other[...]
    for n in range(C):
        at = slice(n * half, (n + 1) * half)
        value = jnp.where(is_first, far, own) if n else jnp.where(is_first, own, far)
        new_first[0, :, at] = first_of(first[0, :, at], value)
        new_second[0, :, at] = second_of(second[0, :, at], value)


def adam(places, mine, other, first, second):
    whole = pl.BlockSpec(memory_space=pltpu.VMEM)
    operands = (places, mine, other, first, second)
    specs = [pl.BlockSpec(memory_space=pltpu.SMEM)] + [whole] * 4
    params = pltpu.CompilerParams(vmem_limit_bytes=5 * 1024 * 1024)
    direction = pl.pallas_call(
        direction_kernel,
        out_shape=jax.ShapeDtypeStruct(first.shape[1:], jnp.bfloat16),
        in_specs=specs,
        out_specs=whole,
        compiler_params=params,
    )(*operands)
    new_first, new_second = pl.pallas_call(
        moments_kernel,
        out_shape=[jax.ShapeDtypeStruct(first.shape, jnp.float32)] * 2,
        in_specs=specs + [whole],
        out_specs=[whole] * 2,
        compiler_params=params,
    )(*operands, direction)
    return new_first, new_second, direction


def place_kernel(places, *refs):
    pieces, out = refs[:-1], refs[-1]
    for i, piece in enumerate(pieces):
        for j in range(len(OFFSETS)):
            out[places[ROWS + i * len(OFFSETS) + j]] = piece[j]


def place_rows(places, pieces):
    count, owned, depth = pieces[0].shape
    whole = pl.BlockSpec(memory_space=pltpu.VMEM)
    return pl.pallas_call(
        place_kernel,
        out_shape=jax.ShapeDtypeStruct((count * len(pieces), owned, depth), jnp.bfloat16),
        in_specs=[pl.BlockSpec(memory_space=pltpu.SMEM)] + [whole] * len(pieces),
        out_specs=whole,
        compiler_params=pltpu.CompilerParams(vmem_limit_bytes=5 * 1024 * 1024),
    )(places, *pieces)


def per_device(gradient, projector, first_moment, second_moment):
    blocks = gradient.shape[1]
    owned = gradient.shape[2]
    width = gradient.shape[3]
    depth, rank_cols = projector.shape
    half = rank_cols // 2
    part = half // GROUPS
    rows = blocks * owned
    dp = lax.axis_index("dp")
    fsdp = lax.axis_index("fsdp")
    places = lax.dynamic_index_in_dim(
        jnp.asarray(all_places()), dp * (X * ZL) + fsdp, 0, keepdims=False
    )
    c = dp % C

    own_grad = gradient.reshape(ZH, rows // ZH, width)
    other_grad = move(own_grad, other_core)
    both = add(own_grad, other_grad)
    own_half = lax.dynamic_slice(projector, (0, c * half), (depth, half))
    own_half = jnp.stack(
        [own_half[:, g * part : (g + 1) * part] for g in range(GROUPS)]
    )
    near = [
        own_half,
        move(own_half, by_core(along_x(-1), along_ring(-1))),
        move(own_half, by_core(along_x(1), along_ring(1))),
        move(own_half, by_core(along_x(2), two_along_ring)),
    ]

    reduced = []
    stacks = stack_near(near, other_grad, places)
    ahead = [move(held, by_core(along_ring(-1), along_x(-1))) for held in stacks]
    behind = [move(held, by_core(along_ring(1), along_x(1))) for held in stacks]
    accs, done = zip(
        *[project(places, (0,), both, [held], None, False) for held in stacks]
    )
    ahead[0] = pass_on(ahead[0], done[0])
    behind[1] = pass_on(behind[1], *done)
    far = [
        move(ahead[0], by_core(along_ring(-1), along_x(-1))),
        move(behind[1], by_core(along_ring(1), along_x(1))),
    ]
    near_two = [ahead[0], behind[0]]
    acc0, _ = project(places, (1, -1), both, near_two, accs[0], False)
    acc1, token = project(places, (-1,), both, [behind[1]], accs[1], False)
    sums0 = project(places, (2,), both, [far[0]], acc0, True, (token,))
    sums1 = project(
        places, (1, 2), both, [ahead[1], far[1]], acc1, True, (sums0[1],)
    )
    for sums in (sums0, sums1):
        total = sums[0]
        for dy in range(1, Y):
            got = move(sums[dy], along_y(OFFSETS[dy]))
            total = total + got.astype(jnp.float32)
        got = move(total[1].astype(jnp.bfloat16), other_half)
        reduced += [total[0], got.astype(jnp.float32)]
    mine, theirs = split(places, reduced)
    other = move(theirs, other_core)
    new_first, new_second, direction = adam(
        places, mine, other, first_moment, second_moment
    )
    basis_other = move(
        collect(list(zip(stacks, ahead, behind, far))), other_core
    )
    basis = jnp.concatenate([*stacks, basis_other], axis=2)
    gathered = jnp.stack(
        [direction]
        + [
            move(direction, by_core(along_line(-o), along_x(-o)))
            for o in OFFSETS[1:]
        ]
    ).reshape(4 * owned, rank_cols)
    pieces = []
    for i, offset in enumerate(OFFSETS):
        value = lax.dot_general(
            gathered,
            basis[i],
            (((1,), (1,)), ((), ())),
            preferred_element_type=jnp.float32,
        ).astype(jnp.bfloat16)
        if offset:
            value = move(value, by_core(along_x(offset), along_line(offset)))
        pieces.append(value.reshape(4, owned, depth))
    result = place_rows(places, pieces)
    update = result.reshape(1, X * ZL * owned, depth)
    return (update, new_first, new_second)


def solution(mesh):
    in_specs = (
        P("dp", None, "fsdp", None),
        P("fsdp", None),
        P("dp", "fsdp", None),
        P("dp", "fsdp", None),
    )
    out_specs = (P("dp", None, "fsdp"), P("dp", "fsdp", None), P("dp", "fsdp", None))
    return jax.shard_map(
        per_device, mesh=mesh, in_specs=in_specs, out_specs=out_specs, check_vma=False
    )
```

```python
import functools

import jax
import jax.numpy as jnp
import numpy as np
from jax import lax
from jax.experimental import pallas as pl
from jax.experimental.pallas import tpu as pltpu
from jax.sharding import PartitionSpec as P

beta_one = 0.9
beta_two = 0.999
bias_one = 1.0 - 0.9**10
bias_two = 1.0 - 0.999**10
epsilon = 1e-08

ZH, Y, C, X, ZL = 2, 4, 2, 4, 4
AXES = ("dp", "fsdp")
OFFSETS = (0, 1, -1, 2)
GROUPS = 2


def linear(zh, y, c, x, zl):
    return (((zh * Y + y) * C + c) * X + x) * ZL + zl


def move(value, place):
    pairs = []
    for zh in range(ZH):
        for y in range(Y):
            for c in range(C):
                for x in range(X):
                    for zl in range(ZL):
                        target = place(zh, y, c, x, zl)
                        pairs.append((linear(zh, y, c, x, zl), linear(*target)))
    return lax.ppermute(value, AXES, pairs)


def along_x(step):
    return lambda zh, y, c, x, zl: (zh, y, c, (x + step) % X, zl)


def along_y(step):
    return lambda zh, y, c, x, zl: (zh, (y + step) % Y, c, x, zl)


def along_ring(step):
    def place(zh, y, c, x, zl):
        z = (zh * ZL + zl + step) % (ZH * ZL)
        return (z // ZL, y, c, x, z % ZL)

    return place


def two_along_ring(zh, y, c, x, zl):
    return along_ring(2 if zl % 2 else -2)(zh, y, c, x, zl)


def along_line(step):
    return lambda zh, y, c, x, zl: (zh, y, c, x, (zl + step) % ZL)


def other_core(zh, y, c, x, zl):
    return (zh, y, 1 - c, x, zl)


def other_half(zh, y, c, x, zl):
    return (1 - zh, y, c, x, zl)


def by_core(first, second):
    def place(zh, y, c, x, zl):
        return (first if c == 0 else second)(zh, y, c, x, zl)

    return place


def block_at(c, x, zl, inner, outer):
    dx, dz = (inner, outer) if c == 0 else (outer, inner)
    return (x + dx) % X * ZL + (zl + dz) % ZL


def places_of(zh, y, c, x, zl):
    blocks = [block_at(c, x, zl, i, o) for o in OFFSETS for i in OFFSETS]
    rows = [block_at(c, x, zl, -i, o) for i in OFFSETS for o in OFFSETS]
    bands = [(y + o) % Y for o in OFFSETS]
    return blocks + bands + [zh, 1 - zh] + rows + [c]


BANDS = len(OFFSETS) ** 2
SLOTS = BANDS + Y
ROWS = SLOTS + ZH
CORE = ROWS + len(OFFSETS) ** 2


def all_places():
    return np.array(
        [
            places_of(zh, y, c, x, zl)
            for zh in range(ZH)
            for y in range(Y)
            for c in range(C)
            for x in range(X)
            for zl in range(ZL)
        ],
        np.int32,
    )


def project_kernel(outers, last, has_acc, after, places, *refs):
    grad, rest = refs[0], refs[1:]
    outs = rest[-(Y if last else 2) :]
    rest = rest[: len(rest) - len(outs) - after]
    if has_acc:
        acc, rest = rest[-1], rest[:-1]
    pieces = [
        (OFFSETS.index(outer) * len(OFFSETS) + i, right, i)
        for outer, right in zip(outers, rest)
        for i in range(len(OFFSETS))
    ]
    depth, width = rest[0].shape[1:]
    band = grad.shape[1] // Y
    for dy in range(Y):
        row = places[BANDS + dy] if last else dy
        at = pl.ds(pl.multiple_of(row * band, 16), band)
        value = None
        for n, right, i in pieces:
            columns = pl.ds(pl.multiple_of(places[n] * depth, depth), depth)
            term = jnp.dot(
                grad[:, at, columns].reshape(ZH * band, depth),
                right[i],
                preferred_element_type=jnp.float32,
            )
            value = term if value is None else value + term
        value = value.reshape(ZH, band, width)
        if has_acc:
            value = value + acc[:, at, :]
        if last:
            for h in range(ZH):
                slot = places[SLOTS + h]
                outs[dy][slot] = value[h].astype(outs[dy].dtype)
        else:
            outs[0][:, at, :] = value
    if not last:
        outs[1][...] = value[0, : outs[1].shape[0], : outs[1].shape[1]]


def project(places, outers, grad, rights, acc, last, after=()):
    depth, width = rights[0].shape[1:]
    half_rows = grad.shape[1]
    count = sum(right.shape[0] for right in rights)
    whole = pl.BlockSpec(memory_space=pltpu.VMEM)
    operands = [grad, *rights] + ([] if acc is None else [acc]) + list(after)
    if last:
        shapes = [
            jax.ShapeDtypeStruct(
                (ZH, half_rows // Y, width), jnp.float32 if dy == 0 else jnp.bfloat16
            )
            for dy in range(Y)
        ]
    else:
        shapes = [
            jax.ShapeDtypeStruct((ZH, half_rows, width), jnp.float32),
            jax.ShapeDtypeStruct((8, 128), jnp.float32),
        ]
    return pl.pallas_call(
        functools.partial(
            project_kernel, outers, last, acc is not None, len(after)
        ),
        out_shape=shapes,
        in_specs=[pl.BlockSpec(memory_space=pltpu.SMEM)] + [whole] * len(operands),
        out_specs=[whole] * len(shapes),
        compiler_params=pltpu.CompilerParams(vmem_limit_bytes=14 * 1024 * 1024),
        cost_estimate=pl.CostEstimate(
            flops=2 * count * ZH * half_rows * depth * width,
            bytes_accessed=2 * count * depth * (2 * half_rows + width),
            transcendentals=0,
        ),
    )(places, *operands)


def stack_kernel(*refs):
    near, outs = refs[: len(OFFSETS)], refs[len(OFFSETS) + 2 :]
    for group, out in enumerate(outs):
        for i, piece in enumerate(near):
            out[i] = piece[group]


def stack_near(near, grad, places):
    groups, depth, width = near[0].shape
    whole = pl.BlockSpec(memory_space=pltpu.VMEM)
    return pl.pallas_call(
        stack_kernel,
        out_shape=[jax.ShapeDtypeStruct((len(near), depth, width), near[0].dtype)]
        * groups,
        in_specs=[whole] * len(near)
        + [pl.BlockSpec(memory_space=pltpu.HBM), pl.BlockSpec(memory_space=pltpu.SMEM)],
        out_specs=[whole] * groups,
        compiler_params=pltpu.CompilerParams(vmem_limit_bytes=5 * 1024 * 1024),
    )(*near, grad, places)


def add_kernel(first, second, out, slots, sems):
    band = slots.shape[1]
    per_half = out.shape[1] // band
    count = out.shape[0] * per_half
    depth = slots.shape[0]

    def copy(n):
        at = (n // per_half, pl.ds((n % per_half) * band, band))
        return pltpu.make_async_copy(
            second.at[at], slots.at[n % depth], sems.at[n % depth]
        )

    for n in range(depth - 1):
        copy(n).start()
    for n in range(count):
        if n + depth - 1 < count:
            copy(n + depth - 1).start()
        copy(n).wait()
        half, row = n // per_half, (n % per_half) * band

        def rows_on(i, carry):
            at = pl.ds(pl.multiple_of(i * 16, 16), 16)
            into = pl.ds(pl.multiple_of(row + i * 16, 16), 16)
            out[half, into, :] = first[half, into, :] + slots[n % depth, at]
            return carry

        lax.fori_loop(0, band // 16, rows_on, 0)


def add(first, second):
    halves, rows, width = first.shape
    band = rows // 4
    whole = pl.BlockSpec(memory_space=pltpu.VMEM)
    return pl.pallas_call(
        add_kernel,
        out_shape=jax.ShapeDtypeStruct(first.shape, first.dtype),
        in_specs=[whole, pl.BlockSpec(memory_space=pltpu.HBM)],
        out_specs=whole,
        scratch_shapes=[
            pltpu.VMEM((3, band, width), first.dtype),
            pltpu.SemaphoreType.DMA((3,)),
        ],
        compiler_params=pltpu.CompilerParams(vmem_limit_bytes=19 * 1024 * 1024),
        cost_estimate=pl.CostEstimate(
            flops=halves * rows * width,
            bytes_accessed=6 * halves * rows * width,
            transcendentals=0,
        ),
    )(first, second)


def pass_on(value, *after):
    main = pl.BlockSpec(memory_space=pltpu.HBM)
    return pl.pallas_call(
        lambda *refs: None,
        out_shape=jax.ShapeDtypeStruct(value.shape, value.dtype),
        in_specs=[main] + [pl.BlockSpec(memory_space=pl.ANY)] * len(after),
        out_specs=main,
        input_output_aliases={0: 0},
        compiler_params=pltpu.CompilerParams(vmem_limit_bytes=1024 * 1024),
    )(value, *after)


def collect_kernel(pieces, groups, *refs):
    ins, out = refs[: pieces * groups], refs[-1]
    part = ins[0].shape[2]
    for n, ref in enumerate(ins):
        group, piece = n // pieces, n % pieces
        out[piece, :, group * part : (group + 1) * part] = ref[0]


def collect(groups, *after):
    arrays = [array for group in groups for array in group]
    _, depth, part = arrays[0].shape
    pieces, width = len(groups[0]), part * len(groups)
    first = pl.BlockSpec((1, depth, part), lambda i: (0, 0, 0))
    one = [pl.BlockSpec((8, 128), lambda i: (0, 0))] * len(after)
    return pl.pallas_call(
        functools.partial(collect_kernel, pieces, len(groups)),
        grid=(1,),
        out_shape=jax.ShapeDtypeStruct((pieces, depth, width), arrays[0].dtype),
        in_specs=[first] * len(arrays) + one,
        out_specs=pl.BlockSpec((pieces, depth, width), lambda i: (0, 0, 0)),
        compiler_params=pltpu.CompilerParams(vmem_limit_bytes=5 * 1024 * 1024),
    )(*arrays, *after)


def split_kernel(groups, places, *refs):
    sums, mine, theirs = refs[:-2], refs[-2], refs[-1]
    owned = mine.shape[0]
    own = pl.ds(pl.multiple_of(places[CORE] * owned, 8), owned)
    other = pl.ds(pl.multiple_of((1 - places[CORE]) * owned, 8), owned)
    part = mine.shape[1] // groups
    for group in range(groups):
        kept, got = sums[2 * group : 2 * group + 2]
        at = slice(group * part, (group + 1) * part)
        mine[:, at] = kept[own, :] + got[own, :]
        theirs[:, at] = kept[other, :] + got[other, :]


def split(places, sums):
    groups = len(sums) // 2
    rows, part = sums[0].shape
    whole = pl.BlockSpec(memory_space=pltpu.VMEM)
    return pl.pallas_call(
        functools.partial(split_kernel, groups),
        out_shape=[jax.ShapeDtypeStruct((rows // C, part * groups), jnp.float32)] * 2,
        in_specs=[pl.BlockSpec(memory_space=pltpu.SMEM)] + [whole] * len(sums),
        out_specs=[whole] * 2,
        compiler_params=pltpu.CompilerParams(vmem_limit_bytes=5 * 1024 * 1024),
    )(places, *sums)


def halves(places, array, n):
    half = array.shape[2] // C
    parts = [array[0, :, m * half : (m + 1) * half] for m in (n, 1 - n)]
    return jnp.where(places[CORE] == 0, parts[0], parts[1])


def first_of(moment, value):
    return beta_one * moment + (1.0 - beta_one) * value


def second_of(moment, value):
    return beta_two * moment + (1.0 - beta_two) * value * value


def direction_kernel(places, mine, other, first, second, out):
    half = mine.shape[1]
    for n, ref in enumerate((mine, other)):
        value = ref[...]
        moment = first_of(halves(places, first, n), value)
        square = second_of(halves(places, second, n), value)
        step = moment / bias_one / (jnp.sqrt(square / bias_two) + epsilon)
        out[:, n * half : (n + 1) * half] = step.astype(out.dtype)


def moments_kernel(places, mine, other, first, second, after, new_first, new_second):
    half = mine.shape[1]
    is_first = places[CORE] == 0
    own, far = mine[...], other[...]
    for n in range(C):
        at = slice(n * half, (n + 1) * half)
        value = jnp.where(is_first, far, own) if n else jnp.where(is_first, own, far)
        new_first[0, :, at] = first_of(first[0, :, at], value)
        new_second[0, :, at] = second_of(second[0, :, at], value)


def adam(places, mine, other, first, second):
    whole = pl.BlockSpec(memory_space=pltpu.VMEM)
    operands = (places, mine, other, first, second)
    specs = [pl.BlockSpec(memory_space=pltpu.SMEM)] + [whole] * 4
    params = pltpu.CompilerParams(vmem_limit_bytes=5 * 1024 * 1024)
    direction = pl.pallas_call(
        direction_kernel,
        out_shape=jax.ShapeDtypeStruct(first.shape[1:], jnp.bfloat16),
        in_specs=specs,
        out_specs=whole,
        compiler_params=params,
    )(*operands)
    new_first, new_second = pl.pallas_call(
        moments_kernel,
        out_shape=[jax.ShapeDtypeStruct(first.shape, jnp.float32)] * 2,
        in_specs=specs + [whole],
        out_specs=[whole] * 2,
        compiler_params=params,
    )(*operands, direction)
    return new_first, new_second, direction


def back_kernel(indices, rows, *refs):
    rights, outs = refs[: -len(indices)], refs[-len(indices) :]
    for i, out in zip(indices, outs):
        at, value = 0, None
        for right in rights:
            width = right.shape[2]
            term = lax.dot_general(
                rows[:, at : at + width],
                right[i],
                (((1,), (1,)), ((), ())),
                preferred_element_type=jnp.float32,
            )
            value = term if value is None else value + term
            at += width
        out[...] = value.astype(out.dtype)


def back(indices, rows, rights):
    depth = rights[0].shape[1]
    whole = pl.BlockSpec(memory_space=pltpu.VMEM)
    return pl.pallas_call(
        functools.partial(back_kernel, indices),
        out_shape=[jax.ShapeDtypeStruct((rows.shape[0], depth), rows.dtype)]
        * len(indices),
        in_specs=[whole] * (1 + len(rights)),
        out_specs=[whole] * len(indices),
        compiler_params=pltpu.CompilerParams(vmem_limit_bytes=7 * 1024 * 1024),
        cost_estimate=pl.CostEstimate(
            flops=2 * len(indices) * rows.size * depth,
            bytes_accessed=4 * len(indices) * rows.shape[1] * depth,
            transcendentals=0,
        ),
    )(rows, *rights)


def place_kernel(places, *refs):
    pieces, out = refs[:-1], refs[-1]
    for i, piece in enumerate(pieces):
        for j in range(len(OFFSETS)):
            out[places[ROWS + i * len(OFFSETS) + j]] = piece[j]


def place_rows(places, pieces):
    count, owned, depth = pieces[0].shape
    whole = pl.BlockSpec(memory_space=pltpu.VMEM)
    return pl.pallas_call(
        place_kernel,
        out_shape=jax.ShapeDtypeStruct((count * len(pieces), owned, depth), jnp.bfloat16),
        in_specs=[pl.BlockSpec(memory_space=pltpu.SMEM)] + [whole] * len(pieces),
        out_specs=whole,
        compiler_params=pltpu.CompilerParams(vmem_limit_bytes=5 * 1024 * 1024),
    )(places, *pieces)


def per_device(gradient, projector, first_moment, second_moment):
    blocks = gradient.shape[1]
    owned = gradient.shape[2]
    width = gradient.shape[3]
    depth, rank_cols = projector.shape
    half = rank_cols // 2
    part = half // GROUPS
    rows = blocks * owned
    dp = lax.axis_index("dp")
    fsdp = lax.axis_index("fsdp")
    places = lax.dynamic_index_in_dim(
        jnp.asarray(all_places()), dp * (X * ZL) + fsdp, 0, keepdims=False
    )
    c = dp % C

    own_grad = gradient.reshape(ZH, rows // ZH, width)
    other_grad = move(own_grad, other_core)
    both = add(own_grad, other_grad)
    own_half = lax.dynamic_slice(projector, (0, c * half), (depth, half))
    own_half = jnp.stack(
        [own_half[:, g * part : (g + 1) * part] for g in range(GROUPS)]
    )
    near = [
        own_half,
        move(own_half, by_core(along_x(-1), along_ring(-1))),
        move(own_half, by_core(along_x(1), along_ring(1))),
        move(own_half, by_core(along_x(2), two_along_ring)),
    ]

    reduced = []
    stacks = stack_near(near, other_grad, places)
    ahead = [move(held, by_core(along_ring(-1), along_x(-1))) for held in stacks]
    behind = [move(held, by_core(along_ring(1), along_x(1))) for held in stacks]
    accs, done = zip(
        *[project(places, (0,), both, [held], None, False) for held in stacks]
    )
    ahead[0] = pass_on(ahead[0], done[0])
    behind[1] = pass_on(behind[1], *done)
    far = [
        move(ahead[0], by_core(along_ring(-1), along_x(-1))),
        move(behind[1], by_core(along_ring(1), along_x(1))),
    ]
    near_two = [ahead[0], behind[0]]
    acc0, _ = project(places, (1, -1), both, near_two, accs[0], False)
    acc1, token = project(places, (-1,), both, [behind[1]], accs[1], False)
    sums0 = project(places, (2,), both, [far[0]], acc0, True, (token,))
    sums1 = project(
        places, (1, 2), both, [ahead[1], far[1]], acc1, True, (sums0[1],)
    )
    for sums in (sums0, sums1):
        total = sums[0]
        for dy in range(1, Y):
            got = move(sums[dy], along_y(OFFSETS[dy]))
            total = total + got.astype(jnp.float32)
        got = move(total[1].astype(jnp.bfloat16), other_half)
        reduced += [total[0], got.astype(jnp.float32)]
    mine, theirs = split(places, reduced)
    other = move(theirs, other_core)
    new_first, new_second, direction = adam(
        places, mine, other, first_moment, second_moment
    )
    basis_other = move(
        collect(list(zip(stacks, ahead, behind, far))), other_core
    )
    gathered = jnp.stack(
        [direction]
        + [
            move(direction, by_core(along_line(-o), along_x(-o)))
            for o in OFFSETS[1:]
        ]
    ).reshape(4 * owned, rank_cols)
    rights = [*stacks, basis_other]
    sent = back((1, 2, 3), gathered, rights)
    values = list(back((0,), gathered, rights)) + [
        move(value, by_core(along_x(offset), along_line(offset)))
        for offset, value in zip(OFFSETS[1:], sent)
    ]
    pieces = [value.reshape(4, owned, depth) for value in values]
    result = place_rows(places, pieces)
    update = result.reshape(1, X * ZL * owned, depth)
    return (update, new_first, new_second)


def solution(mesh):
    in_specs = (
        P("dp", None, "fsdp", None),
        P("fsdp", None),
        P("dp", "fsdp", None),
        P("dp", "fsdp", None),
    )
    out_specs = (P("dp", None, "fsdp"), P("dp", "fsdp", None), P("dp", "fsdp", None))
    return jax.shard_map(
        per_device, mesh=mesh, in_specs=in_specs, out_specs=out_specs, check_vma=False
    )
```
